32 devices in a mesh: ctx: 16 (over z, y, x), fsdp: 2 (over core).
Axes of the slice: x: 2, y: 2, z: 4, core: 2. Of those that a mesh axis runs over, the one named last changes fastest.
Arguments:
- layer_input: bfloat16 [2, 4096, 896], P('fsdp', 'ctx'), may hold values from -6 to 6
- out_cotangent: bfloat16 [2, 4096, 896], P('fsdp', 'ctx'), may hold values from -6 to 6
- span_perm: int32 [16], replicated, may hold values from 0 to 15, each once
- attn_gain: bfloat16 [896], P('fsdp'), may hold values from 0.25 to 1.75
- query_weight: bfloat16 [896, 896], P('fsdp'), may hold values from -0.25 to 0.25
- query_bias: bfloat16 [896], P('fsdp'), may hold values from -3 to 3
- key_weight: bfloat16 [896, 128], P('fsdp'), may hold values from -0.25 to 0.25
- key_bias: bfloat16 [128], P('fsdp'), may hold values from -3 to 3
- value_weight: bfloat16 [896, 128], P('fsdp'), may hold values from -0.1875 to 0.1875
- value_bias: bfloat16 [128], P('fsdp'), may hold values from -0.29882812 to 0.29882812
- output_weight: bfloat16 [896, 896], P('fsdp'), may hold values from -2 to 2
- mlp_gain: bfloat16 [896], P('fsdp'), may hold values from 0.25 to 1.75
- gate_weight: bfloat16 [896, 4864], P('fsdp'), may hold values from -0.1875 to 0.1875
- up_weight: bfloat16 [896, 4864], P('fsdp'), may hold values from -0.1875 to 0.1875
- down_weight: bfloat16 [4864, 896], P('fsdp'), may hold values from -0.078125 to 0.078125
Outputs:
- layer_output: bfloat16 [2, 4096, 896], P('fsdp', 'ctx')
- input_grad: float32 [2, 4096, 896], P('fsdp', 'ctx')
- attn_gain_grad: float32 [896], P('fsdp')
- query_weight_grad: float32 [896, 896], P('fsdp')
- query_bias_grad: float32 [896], P('fsdp')
- key_weight_grad: float32 [896, 128], P('fsdp')
- key_bias_grad: float32 [128], P('fsdp')
- value_weight_grad: float32 [896, 128], P('fsdp')
- value_bias_grad: float32 [128], P('fsdp')
- output_weight_grad: float32 [896, 896], P('fsdp')
- mlp_gain_grad: float32 [896], P('fsdp')
- gate_weight_grad: float32 [896, 4864], P('fsdp')
- up_weight_grad: float32 [896, 4864], P('fsdp')
- down_weight_grad: float32 [4864, 896], P('fsdp')
The draws below stay inside these ranges and needn't reach their ends.
Inputs may be any that keep to these rules, and one draw needn't show every extreme that they name: span_perm is a permutation; index d of ctx holds span span_perm[d] of 128 tokens and then span 2 * 16 - 1 - span_perm[d].
All inputs are finite; a program needn't handle non-finite values.
Results may differ from the reference program's by a relative error of at most 0.028.
Values may be sent and summed in bfloat16 or wider, within the bound.
A program may use at most 256 MiB of HBM per device.

```python
import math
import jax
import jax.numpy as jnp
from jax import lax

D = 896
HEADS = 14
KV_HEADS = 2
HEAD_DIM = 64
FF = 4864
TOK_DEV = 256
SPAN = 128
SEQ = 4096
Q_WIDTH = 896
KV_WIDTH = 128
N_CTX = 16
N_FSDP = 2


def levels(stream_key, shape, pieces, low, largest):
    gain = 1.0
    for position, parts in pieces:
        steps = jax.random.uniform(jax.random.fold_in(jax.random.fold_in(stream_key, 6), position), (parts,), jnp.float32, low / len(pieces), largest / len(pieces))
        gain = gain * jnp.repeat(jnp.exp(steps), shape[position] // parts).reshape((-1,) + (1,) * (len(shape) - 1 - position))
    return gain


def scatter_about(own_key, shape, width, limit, shards=(), held_as=jnp.bfloat16):
    array = width * jax.random.normal(own_key, shape, jnp.float32)
    if shards:
        array = array * levels(own_key, shape, shards, -0.22, 0.18)
    return jnp.clip(array, -limit, limit).astype(held_as)


def setup_inputs(seed: int = 0) -> dict:
    splits = jax.random.split(jax.random.key(seed), 16)
    return {
        "layer_input": scatter_about(splits[0], (N_FSDP, SEQ, D), 1.0, 6.0, ((0, 2), (1, 16))),
        "out_cotangent": scatter_about(splits[1], (N_FSDP, SEQ, D), 1.0, 6.0, ((0, 2), (1, 16))),
        "span_perm": jax.random.permutation(splits[2], N_CTX).astype(jnp.int32),
        "attn_gain": jnp.clip(1.0 + 0.15 * jax.random.normal(splits[3], (D,), jnp.float32), 0.25, 1.75).astype(jnp.bfloat16),
        "query_weight": scatter_about(splits[4], (D, Q_WIDTH), (D // 2) ** -0.5, 0.25, ((0, 2),)),
        "query_bias": scatter_about(splits[5], (Q_WIDTH,), 0.5, 3.0, ((0, 2),)),
        "key_weight": scatter_about(splits[6], (D, KV_WIDTH), (D // 2) ** -0.5, 0.25, ((0, 2),)),
        "key_bias": scatter_about(splits[7], (KV_WIDTH,), 0.5, 3.0, ((0, 2),)),
        "value_weight": scatter_about(splits[8], (D, KV_WIDTH), D ** -0.5, 0.1875, ((0, 2),)),
        "value_bias": scatter_about(splits[9], (KV_WIDTH,), 0.05, 0.29882812, ((0, 2),)),
        "output_weight": scatter_about(splits[10], (Q_WIDTH, D), (max(D // 128, 4)) ** -0.5, 2.0, ((0, 2),)),
        "mlp_gain": jnp.clip(1.0 + 0.15 * jax.random.normal(splits[11], (D,), jnp.float32), 0.25, 1.75).astype(jnp.bfloat16),
        "gate_weight": scatter_about(splits[12], (D, FF), D ** -0.5, 0.1875, ((0, 2),)),
        "up_weight": scatter_about(splits[13], (D, FF), D ** -0.5, 0.1875, ((0, 2),)),
        "down_weight": scatter_about(splits[14], (FF, D), FF ** -0.5, 0.078125, ((0, 2),)),
    }


@jax.custom_vjp
def low(v):
    return lax.optimization_barrier(v.astype(jnp.bfloat16)).astype(jnp.float32)

@jax.custom_vjp
def low_back(v):
    return v

def low_keep(v):
    return (low(v), None)

def low_pass(kept, grad):
    return (grad,)

def back_keep(v):
    return (v, None)

def back_low(kept, grad):
    return (low(grad),)
low.defvjp(low_keep, low_pass)
low_back.defvjp(back_keep, back_low)
EPSILON = 1e-06
THETA_LOG = math.log(1000000.0)
NEGATIVE = -1e+30
HIGHEST = lax.Precision.HIGHEST

def rms_scale(values, gain_vec):
    return values * lax.rsqrt(lax.optimization_barrier(jnp.mean(values * values, axis=-1, keepdims=True)) + EPSILON) * gain_vec

def angle_table(places):
    half_dim = HEAD_DIM // 2
    frequency = jnp.exp(-(2.0 * jnp.arange(half_dim, dtype=jnp.float32) / HEAD_DIM) * THETA_LOG)
    return places.astype(jnp.float32)[:, None] * frequency[None, :]

def rotate(values, angles):
    half_dim = values.shape[-1] // 2
    cosine = jnp.cos(angles)[:, None, :]
    sine_part = jnp.sin(angles)[:, None, :]
    first_half = values[..., :half_dim]
    second = values[..., half_dim:]
    return jnp.concatenate([first_half * cosine - second * sine_part, second * cosine + first_half * sine_part], axis=-1)

def place_table(span_perm):
    row_ids = jnp.arange(SEQ, dtype=jnp.int32)
    owner_dev = (row_ids // TOK_DEV).astype(jnp.int32)
    within = row_ids % TOK_DEV
    first_span = jnp.take(span_perm, owner_dev).astype(jnp.int32)
    span_id = jnp.where(within < SPAN, first_span, 2 * N_CTX - 1 - first_span)
    return (span_id * SPAN + within % SPAN).astype(jnp.int32)

def attention(query_rot, key_rot, value_rot, places):
    group_size = HEADS // KV_HEADS
    block_rows = math.gcd(SEQ, 512)
    score_scale = 1.0 / math.sqrt(HEAD_DIM)
    query_blocks = query_rot.reshape(SEQ // block_rows, block_rows, KV_HEADS, group_size, HEAD_DIM)
    place_blocks = places.reshape(SEQ // block_rows, block_rows)

    def one_block(block_data):
        query_block, query_place = block_data
        raw_scores = jnp.einsum('qhgd,khd->hgqk', query_block, key_rot, precision=HIGHEST)
        scores = score_scale * low_back(raw_scores)
        allowed = query_place[:, None] >= places[None, :]
        weights = low(jax.nn.softmax(jnp.where(allowed, scores, NEGATIVE), axis=-1))
        blended = jnp.einsum('hgqk,khd->qhgd', weights, value_rot, precision=HIGHEST)
        return blended.reshape(block_rows, HEADS * HEAD_DIM)
    return lax.map(jax.checkpoint(one_block), (query_blocks, place_blocks)).reshape(SEQ, HEADS * HEAD_DIM)

def layer(inputs, weights, places, angles):
    attn_gain, query_weight, query_bias, key_weight, key_bias, value_weight, value_bias, output_weight, mlp_gain, gate_weight, up_weight, down_weight = weights
    normed = low(rms_scale(inputs, attn_gain))
    queries = jnp.dot(normed, query_weight, precision=HIGHEST) + query_bias
    key_proj = jnp.dot(normed, key_weight, precision=HIGHEST) + key_bias
    value_proj = jnp.dot(normed, value_weight, precision=HIGHEST) + value_bias
    query_rot = low(rotate(low_back(queries).reshape(SEQ, HEADS, HEAD_DIM), angles))
    key_rot = low(rotate(low_back(key_proj).reshape(SEQ, KV_HEADS, HEAD_DIM), angles))
    value_rot = low(low_back(value_proj)).reshape(SEQ, KV_HEADS, HEAD_DIM)
    mixed = low(low_back(attention(query_rot, key_rot, value_rot, places)))
    middle = inputs + low_back(jnp.dot(mixed, output_weight, precision=HIGHEST))
    normed_two = low(rms_scale(middle, mlp_gain))
    gate_act = low_back(jnp.dot(normed_two, gate_weight, precision=HIGHEST))
    up_act = low_back(jnp.dot(normed_two, up_weight, precision=HIGHEST))
    hidden = low(jax.nn.silu(gate_act) * up_act)
    return middle + jnp.dot(hidden, down_weight, precision=HIGHEST)

def reference(layer_input, out_cotangent, span_perm, attn_gain, query_weight, query_bias, key_weight, key_bias, value_weight, value_bias, output_weight, mlp_gain, gate_weight, up_weight, down_weight):
    places = place_table(span_perm)
    angles = angle_table(places)
    params = tuple((item.astype(jnp.float32) for item in (attn_gain, query_weight, query_bias, key_weight, key_bias, value_weight, value_bias, output_weight, mlp_gain, gate_weight, up_weight, down_weight)))

    def one_sequence(carried, seq_data):
        seq_input, seq_cot = seq_data
        result, pull_back = jax.vjp(lambda inputs, weights: layer(inputs, weights, places, angles), seq_input.astype(jnp.float32), params)
        grad_input, grad_weights = pull_back(seq_cot.astype(jnp.float32))
        carried = tuple((summed + latest for summed, latest in zip(carried, grad_weights)))
        return (carried, (result.astype(jnp.bfloat16), grad_input))
    zeros = tuple((jnp.zeros(item.shape, jnp.float32) for item in params))
    sums, (outputs, input_grads) = lax.scan(one_sequence, zeros, (layer_input, out_cotangent))
    return (outputs, input_grads, sums[0], sums[1], sums[2], sums[3], sums[4], sums[5], sums[6], sums[7], sums[8], sums[9], sums[10], sums[11])
```

```python
import functools
import math

import jax
import jax.numpy as jnp
import numpy as np
from jax import lax
from jax.experimental import pallas as pl
from jax.experimental.pallas import tpu as pltpu
from jax.sharding import PartitionSpec as P

HEADS = 14
KV_HEADS = 2
HEAD_DIM = 64


EPSILON = 1e-06
THETA_LOG = math.log(1000000.0)
NEGATIVE = -1e30


LANE_SHARES = (0.4, 0.4, 0.2)


def lane_orders(ctx_count):
    bits = list(range(ctx_count.bit_length() - 1))
    return (bits, [1, 0] + bits[2:], bits[2:] + bits[:2])


def lane_chunks(units, splits, ctx_count):
    orders = lane_orders(ctx_count)
    third = max(1, round(units * LANE_SHARES[2]))
    first = (units - third + 1) // 2
    counts = (first, units - third - first, third)
    lists = []
    for order, count, parts in zip(orders, counts, splits):
        parts = min(parts, count)
        sizes = [count // parts + (1 if i < count % parts else 0) for i in range(parts)]
        lists.append([(size, order) for size in sizes])
    chunks = []
    start = 0
    for level in range(max(len(items) for items in lists)):
        for items in lists:
            if level < len(items):
                size, order = items[level]
                chunks.append((start, size, order))
                start += size
    return chunks


def bit_of(index, bit):
    return lax.rem(index // (1 << bit), 2)


def exchange_kernel(chunks, ctx_count, fsdp_sum, scatter, gather, *refs):
    stages = ctx_count.bit_length() - 1
    unit = 16 * ctx_count
    refs = list(refs)
    source, result = refs[0], refs[1]
    scratch = refs[2:]
    me = lax.axis_index("ctx")
    core = lax.axis_index("fsdp")
    partners = [me + (1 << b) * (1 - 2 * bit_of(me, b)) for b in range(stages)]
    total = sum(size for _, size, _ in chunks) * unit
    mesh_id = pl.DeviceIdType.MESH

    barrier = pltpu.get_barrier_semaphore()
    for partner in partners:
        pl.semaphore_signal(
            barrier, inc=1, device_id={"ctx": partner}, device_id_type=mesh_id
        )
    if fsdp_sum:
        pl.semaphore_signal(
            barrier, inc=1, device_id={"fsdp": 1 - core}, device_id_type=mesh_id
        )
    pl.semaphore_wait(barrier, stages + (1 if fsdp_sum else 0))

    def rows(start, size):
        return pl.ds(pl.multiple_of(start, 16), size)

    def places(chunk):
        start, size, order = chunk
        low = start * unit
        span = size * unit
        found = []
        for bit in order:
            half = span // 2
            mine = bit_of(me, bit)
            found.append((low + mine * half, low + (1 - mine) * half, half, bit))
            low = low + mine * half
            span = half
        return found, low, span

    plans = [places(chunk) for chunk in chunks]
    pending = []

    def remote(src, dst, sems, c, s, target):
        copy = pltpu.make_async_remote_copy(
            src_ref=src,
            dst_ref=dst,
            send_sem=sems[0].at[c, s],
            recv_sem=sems[1].at[c, s],
            device_id=target,
            device_id_type=mesh_id,
        )
        copy.start()
        pending.append(copy)
        return copy

    def add_rows(own, low, other, low_other, size):
        block = 16 * max(d for d in (1, 2, 3, 4) if (size // 16) % d == 0)

        @pl.loop(0, size // block)
        def _(i):
            here = rows(low + i * block, block)
            own[here, :] = own[here, :] + other[rows(low_other + i * block, block), :]

    if scatter:
        own, landings, local_sems = scratch[0], scratch[1 : 1 + stages], scratch[1 + stages]
        rs_sems = scratch[2 + stages : 4 + stages]
        rest = scratch[4 + stages :]
        if fsdp_sum:
            first_landing, rest = rest[0], rest[1:]
            fs_sems, rest = rest[:2], rest[2:]
        loads, firsts = [], []
        for c, (start, size, _) in enumerate(chunks):
            low, span = start * unit, size * unit
            if fsdp_sum:
                firsts.append(
                    remote(
                        source.at[rows((1 - core) * total + low, span)],
                        first_landing.at[rows(low, span)],
                        fs_sems,
                        c,
                        0,
                        {"fsdp": 1 - core},
                    )
                )
            base = core * total if fsdp_sum else 0
            load = pltpu.make_async_copy(
                source.at[rows(base + low, span)], own.at[rows(low, span)], local_sems.at[c]
            )
            load.start()
            loads.append(load)
        arrivals = {}
        for s in range(stages + 1):
            for c, (start, size, _) in enumerate(chunks):
                found, low_end, span_end = plans[c]
                if s == 0:
                    loads[c].wait()
                    if fsdp_sum:
                        firsts[c].wait_recv()
                        add_rows(own, start * unit, first_landing, start * unit, size * unit)
                else:
                    keep, _, half, _ = found[s - 1]
                    arrivals[c].wait_recv()
                    add_rows(own, keep, landings[s - 1], (start * unit) >> s, half)
                if s < stages:
                    _, send, half, bit = found[s]
                    arrivals[c] = remote(
                        own.at[rows(send, half)],
                        landings[s].at[rows((start * unit) >> (s + 1), half)],
                        rs_sems,
                        c,
                        s,
                        {"ctx": partners[bit]},
                    )
                else:
                    target = low_end if gather else start * 16
                    store = pltpu.make_async_copy(
                        own.at[rows(low_end, span_end)],
                        result.at[rows(target, span_end)],
                        local_sems.at[c],
                    )
                    store.start()
                    loads[c] = store
    else:
        local_sems, rest = scratch[0], scratch[1:]
        loads = []
        for c, (start, size, _) in enumerate(chunks):
            _, low_end, span_end = plans[c]
            store = pltpu.make_async_copy(
                source.at[rows(start * 16, size * 16)],
                result.at[rows(low_end, span_end)],
                local_sems.at[c],
            )
            store.start()
            loads.append(store)
    if gather:
        ag_sems = rest[:2]
        arrivals = {}
        for s in range(stages + 1):
            for c in range(len(chunks)):
                found, _, _ = plans[c]
                if s == 0:
                    loads[c].wait()
                else:
                    arrivals[c].wait_recv()
                if s < stages:
                    keep, _, half, bit = found[stages - 1 - s]
                    region = result.at[rows(keep, half)]
                    arrivals[c] = remote(
                        region, region, ag_sems, c, s, {"ctx": partners[bit]}
                    )
    else:
        for load in loads:
            load.wait()
    for copy in pending:
        copy.wait_send()


def exchange(source, chunks, ctx_count, collective_id, fsdp_sum, scatter, gather):
    stages = ctx_count.bit_length() - 1
    unit = 16 * ctx_count
    columns = source.shape[1]
    total = sum(size for _, size, _ in chunks) * unit
    bf16 = jnp.bfloat16
    count = len(chunks)
    dma = pltpu.SemaphoreType.DMA
    scratch = []
    if scatter:
        scratch.append(pltpu.VMEM((total, columns), bf16))
        scratch += [pltpu.VMEM((total >> (s + 1), columns), bf16) for s in range(stages)]
        scratch += [dma((count,)), dma((count, stages)), dma((count, stages))]
        if fsdp_sum:
            scratch += [pltpu.VMEM((total, columns), bf16), dma((count, 1)), dma((count, 1))]
    else:
        scratch.append(dma((count,)))
    if gather:
        scratch += [dma((count, stages)), dma((count, stages))]
    out_rows = total if gather else total // ctx_count
    return pl.pallas_call(
        functools.partial(exchange_kernel, chunks, ctx_count, fsdp_sum, scatter, gather),
        out_shape=jax.ShapeDtypeStruct((out_rows, columns), bf16),
        in_specs=[pl.BlockSpec(memory_space=pl.ANY)],
        out_specs=pl.BlockSpec(memory_space=pl.ANY),
        scratch_shapes=scratch,
        compiler_params=pltpu.CompilerParams(
            collective_id=collective_id, has_side_effects=True, vmem_limit_bytes=56 * 2**20
        ),
    )(source)


def rms_scale(values, gain_vec):
    return (
        values * lax.rsqrt(jnp.mean(values * values, axis=-1, keepdims=True) + EPSILON) * gain_vec
    )


def swiglu(gate_act, up_act):
    return jax.nn.silu(gate_act) * up_act


def angle_table(places, head_size):
    half_dim = head_size // 2
    frequency = jnp.exp(-(2.0 * jnp.arange(half_dim, dtype=jnp.float32) / head_size) * THETA_LOG)
    return places.astype(jnp.float32)[:, None] * frequency[None, :]


def rotate(values, angles):
    half_dim = values.shape[-1] // 2
    cosine = jnp.cos(angles)[:, None, :]
    sine_part = jnp.sin(angles)[:, None, :]
    first_half = values[..., :half_dim]
    second = values[..., half_dim:]
    return jnp.concatenate(
        [first_half * cosine - second * sine_part, second * cosine + first_half * sine_part],
        axis=-1,
    )


def place_table(span_perm, owner_dev, within, tok_rows, ctx_count):
    matches = owner_dev[:, None] == jnp.arange(ctx_count, dtype=jnp.int32)[None, :]
    first_span = jnp.sum(jnp.where(matches, span_perm[None, :], 0), axis=1)
    half_rows = tok_rows // 2
    span_id = jnp.where(within < half_rows, first_span, 2 * ctx_count - 1 - first_span)
    return span_id * half_rows + within % half_rows


def gathered_order(chunks, ctx_count):
    owners, tokens = [], []
    for start, size, order in chunks:
        slots = np.arange(ctx_count)
        device = np.zeros(ctx_count, np.int64)
        for k, bit in enumerate(order):
            device |= ((slots >> (len(order) - 1 - k)) & 1) << bit
        owners.append(np.repeat(device, size * 16))
        tokens.append(np.tile(np.arange(start * 16, (start + size) * 16), ctx_count))
    return np.concatenate(owners).astype(np.int32), np.concatenate(tokens).astype(np.int32)


def body(
    layer_input,
    out_cotangent,
    span_perm,
    attn_gain,
    query_weight,
    query_bias,
    key_weight,
    key_bias,
    value_weight,
    value_bias,
    output_weight,
    mlp_gain,
    gate_weight,
    up_weight,
    down_weight,
):
    f32 = jnp.float32
    bf16 = jnp.bfloat16
    tok_rows = layer_input.shape[1]
    ctx_count = lax.axis_size("ctx")
    ctx_index = lax.axis_index("ctx")
    group_size = HEADS // KV_HEADS
    kv_width = KV_HEADS * HEAD_DIM
    q_width = HEADS * HEAD_DIM
    score_scale = 1.0 / math.sqrt(HEAD_DIM)
    kv_chunks = lane_chunks(tok_rows // 16, (1, 1, 1), ctx_count)
    key_owner, key_token = gathered_order(kv_chunks, ctx_count)
    place_all = place_table(
        span_perm, jnp.asarray(key_owner), jnp.asarray(key_token), tok_rows, ctx_count
    )
    own_rows = jnp.arange(tok_rows, dtype=jnp.int32)
    place_mine = place_table(
        span_perm, jnp.full((tok_rows,), ctx_index), own_rows, tok_rows, ctx_count
    )
    angles = angle_table(place_mine, HEAD_DIM)
    (
        gain_one,
        weight_query,
        bias_query,
        weight_key,
        bias_key,
        weight_value,
        bias_value,
        weight_out,
    ) = (
        lax.all_gather(attn_gain, "fsdp", axis=0, tiled=True),
        lax.all_gather(query_weight, "fsdp", axis=0, tiled=True),
        lax.all_gather(query_bias, "fsdp", axis=0, tiled=True),
        lax.all_gather(key_weight, "fsdp", axis=0, tiled=True),
        lax.all_gather(key_bias, "fsdp", axis=0, tiled=True),
        lax.all_gather(value_weight, "fsdp", axis=0, tiled=True),
        lax.all_gather(value_bias, "fsdp", axis=0, tiled=True),
        lax.all_gather(output_weight, "fsdp", axis=0, tiled=True),
    )
    inputs = layer_input[0].astype(f32)
    normed = rms_scale(inputs, gain_one.astype(f32)).astype(bf16)
    queries = jnp.dot(normed, weight_query, preferred_element_type=f32) + bias_query.astype(f32)
    key_proj = jnp.dot(normed, weight_key, preferred_element_type=f32) + bias_key.astype(f32)
    value_proj = jnp.dot(normed, weight_value, preferred_element_type=f32) + bias_value.astype(f32)
    query_rot = rotate(queries.reshape(tok_rows, HEADS, HEAD_DIM), angles).astype(bf16)
    query_rot = query_rot.reshape(tok_rows, KV_HEADS, group_size, HEAD_DIM)
    key_rot = rotate(key_proj.reshape(tok_rows, KV_HEADS, HEAD_DIM), angles).astype(bf16)
    kv_local = jnp.concatenate(
        [key_rot.reshape(tok_rows, kv_width), value_proj.astype(bf16)], axis=1
    )

    def split_piece(shard_rows):
        piece_rows = shard_rows.shape[0]
        block_rows = math.gcd(piece_rows, 512)
        key_blocks = shard_rows[:, :kv_width].reshape(
            piece_rows // block_rows, block_rows, KV_HEADS, HEAD_DIM
        )
        value_blocks = shard_rows[:, kv_width:].reshape(
            piece_rows // block_rows, block_rows, KV_HEADS, HEAD_DIM
        )
        key_places = place_all.reshape(piece_rows // block_rows, block_rows)
        return (piece_rows, block_rows, (key_blocks, value_blocks, key_places))

    start_state = (
        jnp.full((KV_HEADS, group_size, tok_rows), NEGATIVE, f32),
        jnp.zeros((KV_HEADS, group_size, tok_rows), f32),
        jnp.zeros((KV_HEADS, group_size, tok_rows, HEAD_DIM), f32),
    )
    carried = start_state
    kv_all = exchange(kv_local, kv_chunks, ctx_count, 1, False, False, True)
    piece_rows, block_rows, blocks = split_piece(kv_all)

    def attend_block(inner, block_data):
        run_max, run_sum, run_out = inner
        key_block, value_block, key_place = block_data
        raw_scores = jnp.einsum("qhgd,khd->hgqk", query_rot, key_block, preferred_element_type=f32)
        allowed = place_mine[:, None] >= key_place[None, :]
        scores = jnp.where(allowed, score_scale * raw_scores, NEGATIVE)
        new_max = jnp.maximum(run_max, jnp.max(scores, axis=-1))
        factor = jnp.exp(run_max - new_max)
        weights = jnp.where(allowed, jnp.exp(scores - new_max[..., None]), 0.0)
        run_sum = factor * run_sum + jnp.sum(weights, axis=-1)
        run_out = factor[..., None] * run_out + jnp.einsum(
            "hgqk,khd->hgqd", weights.astype(bf16), value_block, preferred_element_type=f32
        )
        return ((new_max, run_sum, run_out), None)

    carried, _ = lax.scan(attend_block, carried, blocks)
    run_max, run_sum, run_out = carried
    attn_heads = run_out / run_sum[..., None]
    log_total = run_max + jnp.log(run_sum)
    mixed = jnp.transpose(attn_heads, (2, 0, 1, 3)).reshape(tok_rows, q_width).astype(bf16)
    middle = inputs + jnp.dot(mixed, weight_out, preferred_element_type=f32)
    gain_two, weight_gate, weight_up, weight_down = (
        lax.all_gather(mlp_gain, "fsdp", axis=0, tiled=True),
        lax.all_gather(gate_weight, "fsdp", axis=0, tiled=True),
        lax.all_gather(up_weight, "fsdp", axis=0, tiled=True),
        lax.all_gather(down_weight, "fsdp", axis=0, tiled=True),
    )
    normed_two = rms_scale(middle, gain_two.astype(f32)).astype(bf16)
    gate_act = jnp.dot(normed_two, weight_gate, preferred_element_type=f32)
    up_act = jnp.dot(normed_two, weight_up, preferred_element_type=f32)
    hidden = swiglu(gate_act, up_act).astype(bf16)
    layer_output = (middle + jnp.dot(hidden, weight_down, preferred_element_type=f32)).astype(bf16)
    out_grad = out_cotangent[0]
    grad_down = jnp.einsum("tf,td->fd", hidden, out_grad, preferred_element_type=f32)
    grad_hidden = jnp.einsum("td,fd->tf", out_grad, weight_down, preferred_element_type=f32)
    grad_gate, grad_up = jax.vjp(swiglu, gate_act, up_act)[1](grad_hidden)
    grad_gate = grad_gate.astype(bf16)
    grad_up = grad_up.astype(bf16)
    grad_wgate = jnp.einsum("td,tf->df", normed_two, grad_gate, preferred_element_type=f32)
    grad_wup = jnp.einsum("td,tf->df", normed_two, grad_up, preferred_element_type=f32)
    grad_normed_two = jnp.einsum(
        "tf,df->td", grad_gate, weight_gate, preferred_element_type=f32
    ) + jnp.einsum("tf,df->td", grad_up, weight_up, preferred_element_type=f32)
    grad_middle_part, grad_gain_two = jax.vjp(rms_scale, middle, gain_two.astype(f32))[1](
        grad_normed_two
    )
    grad_middle = out_grad.astype(f32) + grad_middle_part
    grad_branch = grad_middle.astype(bf16)
    grad_wout = jnp.einsum("tq,td->qd", mixed, grad_branch, preferred_element_type=f32)
    grad_mixed = jnp.einsum(
        "td,qd->tq", grad_branch, weight_out, preferred_element_type=f32
    ).astype(bf16)
    grad_heads = jnp.transpose(
        grad_mixed.reshape(tok_rows, KV_HEADS, group_size, HEAD_DIM), (1, 2, 0, 3)
    )
    delta = jnp.sum(grad_heads.astype(f32) * attn_heads, axis=-1)
    grad_query_acc = jnp.zeros((KV_HEADS, group_size, tok_rows, HEAD_DIM), f32)

    def attend_back(grad_query, block_data):
        key_block, value_block, key_place = block_data
        raw_scores = jnp.einsum("qhgd,khd->hgqk", query_rot, key_block, preferred_element_type=f32)
        allowed = place_mine[:, None] >= key_place[None, :]
        weights = jnp.where(allowed, jnp.exp(score_scale * raw_scores - log_total[..., None]), 0.0)
        grad_value = jnp.einsum(
            "hgqk,hgqd->khd", weights.astype(bf16), grad_heads, preferred_element_type=f32
        )
        grad_weights = jnp.einsum(
            "hgqd,khd->hgqk", grad_heads, value_block, preferred_element_type=f32
        )
        grad_scores = (weights * (grad_weights - delta[..., None]) * score_scale).astype(bf16)
        grad_query = grad_query + jnp.einsum(
            "hgqk,khd->hgqd", grad_scores, key_block, preferred_element_type=f32
        )
        grad_key = jnp.einsum("hgqk,qhgd->khd", grad_scores, query_rot, preferred_element_type=f32)
        joined = jnp.concatenate(
            [grad_key.reshape(block_rows, kv_width), grad_value.reshape(block_rows, kv_width)],
            axis=1,
        )
        return (grad_query, joined)

    grad_query_acc, joined_blocks = lax.scan(attend_back, grad_query_acc, blocks)
    grad_kv_acc = joined_blocks.reshape(piece_rows, 2 * kv_width)
    grad_query_acc, grad_kv_all = (grad_query_acc, grad_kv_acc)
    grad_kv = exchange(
        grad_kv_all.astype(bf16), kv_chunks, ctx_count, 2, False, True, False
    ).astype(f32)
    grad_query_rot = jnp.transpose(grad_query_acc, (2, 0, 1, 3)).reshape(tok_rows, HEADS, HEAD_DIM)
    grad_query = rotate(grad_query_rot, -angles).reshape(tok_rows, q_width).astype(bf16)
    grad_key = rotate(grad_kv[:, :kv_width].reshape(tok_rows, KV_HEADS, HEAD_DIM), -angles)
    grad_key = grad_key.reshape(tok_rows, kv_width).astype(bf16)
    grad_value = grad_kv[:, kv_width:].astype(bf16)
    grad_wquery = jnp.einsum("tc,tq->cq", normed, grad_query, preferred_element_type=f32)
    grad_wkey = jnp.einsum("tc,tq->cq", normed, grad_key, preferred_element_type=f32)
    grad_wvalue = jnp.einsum("tc,tq->cq", normed, grad_value, preferred_element_type=f32)
    grad_bquery = jnp.sum(grad_query.astype(f32), axis=0)
    grad_bkey = jnp.sum(grad_key.astype(f32), axis=0)
    grad_bvalue = jnp.sum(grad_value.astype(f32), axis=0)
    grad_normed = (
        jnp.einsum("tq,cq->tc", grad_query, weight_query, preferred_element_type=f32)
        + jnp.einsum("tq,cq->tc", grad_key, weight_key, preferred_element_type=f32)
        + jnp.einsum("tq,cq->tc", grad_value, weight_value, preferred_element_type=f32)
    )
    grad_input_part, grad_gain_one = jax.vjp(rms_scale, inputs, gain_one.astype(f32))[1](
        grad_normed
    )
    input_grad = grad_middle + grad_input_part
    width = layer_input.shape[2]
    half = width // 2

    def halves(array):
        return array.astype(bf16).reshape(2, array.shape[0] // 2, *array.shape[1:])

    gate_parts, up_parts = halves(grad_wgate), halves(grad_wup)
    whole_blocks = gate_parts.shape[2] // width
    body_cols = whole_blocks * width
    tail_cols = gate_parts.shape[2] - body_cols
    kv_rows = half * kv_width // width
    vectors = jnp.concatenate(
        [
            halves(item)
            for item in (grad_gain_one, grad_bquery, grad_gain_two, grad_bkey, grad_bvalue)
        ],
        axis=1,
    )
    vectors = jnp.pad(vectors, ((0, 0), (0, 16 * width - vectors.shape[1]))).reshape(2, 16, width)
    value_rows = halves(grad_wvalue).reshape(2, width // kv_width, kv_rows, kv_width)
    pieces = [halves(grad_down)]
    for parts in (gate_parts, up_parts):
        pieces += [parts[:, :, i * width : (i + 1) * width] for i in range(whole_blocks)]
    pieces.append(
        jnp.concatenate(
            [gate_parts[:, :, body_cols:], up_parts[:, :, body_cols:], halves(grad_wkey)], axis=2
        )
    )
    pieces += [halves(grad_wquery), halves(grad_wout)]
    pieces.append(jnp.concatenate([value_rows[:, i] for i in range(width // kv_width)], axis=2))
    pieces.append(vectors)
    used = sum(piece.shape[1] for piece in pieces)
    unit = 16 * ctx_count
    padded = -(-used // unit) * unit
    if padded > used:
        pieces.append(jnp.zeros((2, padded - used, width), bf16))
    packed = jnp.concatenate(pieces, axis=1).reshape(2 * padded, width)
    chunks = lane_chunks(padded // unit, (4, 4, 2), ctx_count)
    summed = exchange(packed, chunks, ctx_count, 3, True, True, True)
    ff_half = grad_down.shape[0] // 2
    total_down = summed[:ff_half].astype(f32)
    at = ff_half
    blocks_of = []
    for i in range(2 * whole_blocks + 3):
        blocks_of.append(summed[at : at + half])
        at += half
    tail = blocks_of[2 * whole_blocks]
    total_gate = jnp.concatenate(
        blocks_of[:whole_blocks] + [tail[:, :tail_cols]], axis=1
    ).astype(f32)
    total_up = jnp.concatenate(
        blocks_of[whole_blocks : 2 * whole_blocks] + [tail[:, tail_cols : 2 * tail_cols]], axis=1
    ).astype(f32)
    total_wkey = tail[:, 2 * tail_cols :].astype(f32)
    total_wquery = blocks_of[2 * whole_blocks + 1].astype(f32)
    total_wout = blocks_of[2 * whole_blocks + 2].astype(f32)
    value_sum = summed[at : at + kv_rows]
    total_wvalue = jnp.concatenate(
        [value_sum[:, i * kv_width : (i + 1) * kv_width] for i in range(width // kv_width)], axis=0
    ).astype(f32)
    at += kv_rows
    flat = summed[at : at + 16].reshape(16 * width).astype(f32)
    kv_half = kv_width // 2
    total_gain_one = flat[:half]
    total_bquery = flat[half : 2 * half]
    total_gain_two = flat[2 * half : 3 * half]
    total_bkey = flat[3 * half : 3 * half + kv_half]
    total_bvalue = flat[3 * half + kv_half : 3 * half + 2 * kv_half]
    return (
        layer_output[None],
        input_grad[None],
        total_gain_one,
        total_wquery,
        total_bquery,
        total_wkey,
        total_bkey,
        total_wvalue,
        total_bvalue,
        total_wout,
        total_gain_two,
        total_gate,
        total_up,
        total_down,
    )


def solution(mesh):
    placed = (
        P("fsdp", "ctx", None),
        P("fsdp", "ctx", None),
        P(),
        P("fsdp"),
        P("fsdp", None),
        P("fsdp"),
        P("fsdp", None),
        P("fsdp"),
        P("fsdp", None),
        P("fsdp"),
        P("fsdp", None),
        P("fsdp"),
        P("fsdp", None),
        P("fsdp", None),
        P("fsdp", None),
    )
    return jax.shard_map(
        body,
        mesh=mesh,
        in_specs=placed,
        out_specs=(
            P("fsdp", "ctx", None),
            P("fsdp", "ctx", None),
            P("fsdp"),
            P("fsdp", None),
            P("fsdp"),
            P("fsdp", None),
            P("fsdp"),
            P("fsdp", None),
            P("fsdp"),
            P("fsdp", None),
            P("fsdp"),
            P("fsdp", None),
            P("fsdp", None),
            P("fsdp", None),
        ),
        check_vma=False,
    )
```
